32 devices in a mesh: rep: 4 (over x, core), ep: 8 (over z, y).
Axes of the slice: x: 2, y: 2, z: 4, core: 2. Of those that a mesh axis runs over, the one named last changes fastest.
Arguments:
- tokens: bfloat16 [4096, 2048], P(('rep', 'ep')), may hold values from -6 to 6
- expert_ids: int32 [4096, 8], P(('rep', 'ep')), may hold values from 0 to 31, as said below
- route_weight: float32 [4096, 8], P(('rep', 'ep')), may hold values from 0.05 to 1
- hot_plan: int32 [8], replicated, may hold values from 0 to 3, as said below
- gate_proj: bfloat16 [32, 2048, 768], P(('rep', 'ep')), may hold values from -0.125 to 0.125
- up_proj: bfloat16 [32, 2048, 768], P(('rep', 'ep')), may hold values from -0.125 to 0.125
- down_proj: bfloat16 [32, 768, 2048], P(('rep', 'ep')), may hold values from -0.21875 to 0.21875
Outputs:
- layer_out: bfloat16 [4096, 2048], P(('rep', 'ep'))
- served_load: float32 [32], replicated
The draws below stay inside these ranges and needn't reach their ends.
Inputs may be any that keep to these rules, and one draw needn't show every extreme that they name: `expert_ids`: within the rows of one device (aligned blocks of 128 tokens) a hot expert is named at most 64 times and any other expert at most 24 times. Some expert that is not hot is named exactly 24 times in every block, and the hot expert of some column exactly 64 times in every block. Expert hot_plan[c] * 8 + c is the hot expert of column c.
All inputs are finite; a program needn't handle non-finite values.
Results may differ from the reference program's by a relative error of at most 0.0057.
Values may be sent and summed in bfloat16 or wider, within the bound.
A program may use at most 128 MiB of HBM per device.

```python
import math
import jax
import jax.numpy as jnp
from jax import lax

D = 2048
FF = 768
TOPK = 8
TOK_DEV = 128
EXPERTS = 32
HOT = 8
TOKENS = 4096
CAP = 24
HOT_CAP = 64


def plan_rows(key):
    return jax.random.randint(jax.random.fold_in(key, 11), (HOT,), 0, EXPERTS // HOT).astype(jnp.int32)


def draw_hot_plan(key, part):
    return plan_rows(key)


def draw_expert_ids(key, part):
    hot_rows = plan_rows(key)
    expert_range = jnp.arange(EXPERTS, dtype=jnp.int32)
    hot_flag = expert_range // HOT == hot_rows[expert_range % HOT]
    maxima = jnp.where(hot_flag, HOT_CAP, CAP).astype(jnp.int32)
    total_units = (EXPERTS - HOT) * CAP + HOT * HOT_CAP
    routed = TOK_DEV * TOPK
    removed = total_units - routed
    unit_expert = jnp.repeat(expert_range, maxima, total_repeat_length=total_units).astype(jnp.int32)
    cool_list = jnp.nonzero(jnp.logical_not(hot_flag), size=EXPERTS - HOT, fill_value=0)[0].astype(jnp.int32)
    cool_pick = cool_list[jax.random.randint(jax.random.fold_in(key, 12), (), 0, EXPERTS - HOT)]
    hot_column = jax.random.randint(jax.random.fold_in(key, 13), (), 0, HOT)
    hot_pick = hot_rows[hot_column] * HOT + hot_column
    protected = (unit_expert == cool_pick) | (unit_expert == hot_pick)
    score_span = (2 ** 31 - 1) // total_units - 1
    half_span = score_span // 2
    unit_range = jnp.arange(total_units, dtype=jnp.int32)
    row_favour = jax.random.randint(jax.random.fold_in(key, 15), (EXPERTS // HOT, EXPERTS), 0, 8) == 0

    def one_device(index):
        dev_key = jax.random.fold_in(jax.random.fold_in(key, 14), index)
        row_index = index // HOT
        favoured = row_favour[row_index][unit_expert]
        raw_scores = jax.random.randint(jax.random.fold_in(dev_key, 1), (total_units,), 0, half_span)
        raw_scores = raw_scores + jnp.where(favoured, 0, half_span).astype(jnp.int32)
        scores = raw_scores * total_units + unit_range
        scores = jnp.where(protected, score_span * total_units + unit_range, scores)
        removal_order = jnp.argsort(scores, stable=True)
        kept_mask = jnp.ones((total_units,), jnp.bool_).at[removal_order[:removed]].set(False)
        kept_idx = jnp.nonzero(kept_mask, size=routed, fill_value=0)[0]
        id_table = unit_expert[kept_idx].reshape(TOPK, TOK_DEV).T
        token_perm = jax.random.permutation(jax.random.fold_in(dev_key, 2), TOK_DEV)
        id_table = id_table[token_perm]
        slot_scores = jax.random.randint(jax.random.fold_in(dev_key, 3), (TOK_DEV, TOPK), 0, 2 ** 20) * TOPK + jnp.arange(TOPK, dtype=jnp.int32)[None, :]
        slot_order = jnp.argsort(slot_scores, axis=1, stable=True)
        return jnp.take_along_axis(id_table, slot_order, axis=1)
    device_range = jnp.arange(TOKENS // TOK_DEV, dtype=jnp.int32)
    return jax.vmap(one_device)(device_range).reshape(TOKENS, TOPK).astype(jnp.int32)


def shard_levels(own_key, shape, cuts, least, high):
    def one(axis_at, blocks):
        heights = jax.random.uniform(jax.random.fold_in(jax.random.fold_in(own_key, 6), axis_at), (blocks,), jnp.float32, least / len(cuts), high / len(cuts))
        return jnp.repeat(jnp.exp(heights), shape[axis_at] // blocks).reshape((-1,) + (1,) * (len(shape) - axis_at - 1))

    loudness = one(*cuts[0])
    for cut in cuts[1:]:
        loudness = loudness * one(*cut)
    return loudness


def noise(stream_key, dims, width, reach, shards=(), kind=jnp.bfloat16):
    values = width * jax.random.normal(stream_key, dims, jnp.float32)
    if shards:
        values = values * shard_levels(stream_key, dims, shards, -0.22, 0.18)
    return jnp.clip(values, -reach, reach).astype(kind)


def setup_inputs(seed: int = 0) -> dict:
    streams_of = jax.random.split(jax.random.key(seed), 8)
    tokens = noise(streams_of[0], (TOKENS, D), 1.0, 6.0, ((0, 32),))
    expert_ids = draw_expert_ids(jax.random.fold_in(streams_of[7], 71), 0)
    route_weight = jnp.clip(jnp.exp(math.log(1.0) - 2.9957323 * jax.random.uniform(streams_of[2], (TOKENS, TOPK), jnp.float32) ** shard_levels(streams_of[2], (TOKENS, TOPK), ((0, 32),), -0.2, 0.2)), 0.05, 1.0)
    hot_plan = draw_hot_plan(jax.random.fold_in(streams_of[7], 71), 0)
    gate_proj = noise(streams_of[4], (EXPERTS, D, FF), D ** -0.5, 0.125, ((0, 32),))
    up_proj = noise(streams_of[5], (EXPERTS, D, FF), D ** -0.5, 0.125, ((0, 32),))
    down_proj = noise(streams_of[6], (EXPERTS, FF, D), FF ** -0.5, 0.21875, ((0, 32),))
    return {"tokens": tokens, "expert_ids": expert_ids, "route_weight": route_weight, "hot_plan": hot_plan, "gate_proj": gate_proj, "up_proj": up_proj, "down_proj": down_proj}


def reference(tokens, expert_ids, route_weight, hot_plan, gate_proj, up_proj, down_proj):
    flat_ids = expert_ids.reshape(-1)
    routed = flat_ids.shape[0]
    experts = gate_proj.shape[0]
    devices = tokens.shape[0] // TOK_DEV
    expert_range = jnp.arange(experts, dtype=jnp.int32)
    hot_flag = (expert_range // HOT) == hot_plan[expert_range % HOT]
    row_ids = flat_ids.reshape(experts // HOT, -1)

    def count_row(ids):
        return jnp.sum((ids[:, None] == expert_range[None, :]).astype(jnp.int32), axis=0, dtype=jnp.int32)

    row_counts = lax.map(count_row, row_ids)
    counts = jnp.sum(row_counts, axis=0, dtype=jnp.int32)
    hot_expert = (hot_plan * HOT + jnp.arange(HOT, dtype=jnp.int32)).astype(jnp.int32)
    copy_rows = row_counts[:, hot_expert].reshape(-1)
    served = jnp.where(hot_flag, jnp.zeros_like(counts), counts) + copy_rows
    served_load = served.astype(jnp.float32) / jnp.float32(TOK_DEV * TOPK)

    shares = route_weight / jnp.sum(route_weight, axis=1, keepdims=True)
    flat_shares = shares.reshape(-1)

    def make_step(bound_rows):
        def one_expert(summed, expert):
            picked = jnp.nonzero(flat_ids == expert, size=bound_rows, fill_value=routed)[0].astype(jnp.int32)
            living = picked < routed
            safe_idx = jnp.where(living, picked, 0).astype(jnp.int32)
            token_idx = (safe_idx // TOPK).astype(jnp.int32)
            chosen = tokens[token_idx]
            gate_in = jnp.dot(chosen, gate_proj[expert], preferred_element_type=jnp.float32)
            up_in = jnp.dot(chosen, up_proj[expert], preferred_element_type=jnp.float32)
            hidden = (jax.nn.silu(gate_in) * up_in).astype(jnp.bfloat16)
            result = jnp.dot(hidden, down_proj[expert], preferred_element_type=jnp.float32).astype(jnp.bfloat16)
            weighted = flat_shares[safe_idx][:, None] * result.astype(jnp.float32)
            target = jnp.where(living, token_idx, tokens.shape[0]).astype(jnp.int32)
            summed = summed.at[target].add(weighted, mode="drop")
            return summed, None
        return one_expert

    cool_list = jnp.nonzero(jnp.logical_not(hot_flag), size=experts - HOT, fill_value=0)[0].astype(jnp.int32)
    initial = jnp.zeros((tokens.shape[0], tokens.shape[1]), jnp.float32)
    summed, _ = lax.scan(make_step(CAP * devices), initial, cool_list)
    summed, _ = lax.scan(make_step(HOT_CAP * devices), summed, hot_expert)
    return summed.astype(jnp.bfloat16), served_load
```

```python
import functools

import jax
import jax.numpy as jnp
from jax import lax
from jax.experimental import pallas as pl
from jax.experimental.pallas import tpu as pltpu
from jax.sharding import PartitionSpec as P

AXES = ("rep", "ep")


def expert_kernel(cap, ids_ref, share_ref, x_ref, gate_ref, up_ref, down_ref, out_ref, sel, res):
    blocks, top, rows = ids_ref.shape
    me = (lax.axis_index("rep") * lax.axis_size("ep") + lax.axis_index("ep")).astype(jnp.float32)
    earlier = lax.broadcasted_iota(jnp.int32, (rows, rows), 0) < lax.broadcasted_iota(
        jnp.int32, (rows, rows), 1
    )
    earlier = earlier.astype(jnp.bfloat16)
    slots = lax.broadcasted_iota(jnp.int32, (cap, rows), 0).astype(jnp.float32)
    picks = []
    scales = []
    for b in range(blocks):
        match = ids_ref[b] == me
        weight = jnp.sum(jnp.where(match, share_ref[b], 0.0), axis=0, keepdims=True)
        named = jnp.max(match.astype(jnp.float32), axis=0, keepdims=True)
        before = jnp.dot(
            jnp.broadcast_to(named, (8, rows)).astype(jnp.bfloat16),
            earlier,
            preferred_element_type=jnp.float32,
        )[0:1]
        hit = (slots == before) & (named > 0.0)
        pick = jnp.where(hit, 1.0, 0.0)
        picks.append(pick.astype(jnp.bfloat16))
        scales.append(jnp.sum(pick * weight, axis=1, keepdims=True))
        sel[b * cap : (b + 1) * cap, :] = jnp.dot(
            picks[b], x_ref[b], preferred_element_type=jnp.float32
        ).astype(jnp.bfloat16)
    gate_in = jnp.dot(sel[...], gate_ref[...], preferred_element_type=jnp.float32)
    up_in = jnp.dot(sel[...], up_ref[...], preferred_element_type=jnp.float32)
    hidden = (gate_in / (1.0 + jnp.exp(-gate_in)) * up_in).astype(jnp.bfloat16)
    done = jnp.dot(hidden, down_ref[...], preferred_element_type=jnp.float32)
    for b in range(blocks):
        part = slice(b * cap, (b + 1) * cap)
        res[part, :] = (done[part] * scales[b]).astype(jnp.bfloat16)
    for b in range(blocks):
        out_ref[b] = lax.dot_general(
            picks[b],
            res[b * cap : (b + 1) * cap, :],
            (((0,), (0,)), ((), ())),
            preferred_element_type=jnp.float32,
        ).astype(jnp.bfloat16)


def run_expert(x, ids, shares, gate, up, down, cap):
    blocks, rows, width = x.shape
    top = ids.shape[1]
    hidden = gate.shape[1]
    group = 8 if blocks % 8 == 0 else 1
    whole = lambda shape: pl.BlockSpec(shape, lambda i: (0, 0), pipeline_mode=pl.Buffered(1))
    return pl.pallas_call(
        functools.partial(expert_kernel, cap),
        out_shape=jax.ShapeDtypeStruct(x.shape, jnp.bfloat16),
        grid=(blocks // group,),
        in_specs=[
            pl.BlockSpec((group, top, rows), lambda i: (i, 0, 0)),
            pl.BlockSpec((group, top, rows), lambda i: (i, 0, 0)),
            pl.BlockSpec((group, rows, width), lambda i: (i, 0, 0)),
            whole(gate.shape),
            whole(up.shape),
            whole(down.shape),
        ],
        out_specs=pl.BlockSpec((group, rows, width), lambda i: (i, 0, 0)),
        scratch_shapes=[
            pltpu.VMEM((group * cap, width), jnp.bfloat16),
            pltpu.VMEM((group * cap, width), jnp.bfloat16),
        ],
        compiler_params=pltpu.CompilerParams(vmem_limit_bytes=56 * 1024 * 1024),
        cost_estimate=pl.CostEstimate(
            flops=6 * blocks * cap * width * hidden,
            bytes_accessed=4 * blocks * rows * width + 6 * width * hidden,
            transcendentals=blocks * cap * hidden,
        ),
    )(ids, shares, x, gate, up, down)


def load_of(all_ids, hot_plan, n_rep, n_ep, routed):
    devices = n_rep * n_ep
    expert_range = jnp.arange(devices, dtype=jnp.int32)
    by_row = all_ids.reshape(n_rep, 1, -1)
    row_counts = jnp.sum(
        (by_row == expert_range.astype(jnp.float32)[None, :, None]).astype(jnp.float32), axis=2
    ).astype(jnp.int32)
    hot_flag = (expert_range // n_ep) == jnp.tile(hot_plan, n_rep)
    counts = jnp.sum(row_counts, axis=0, dtype=jnp.int32)
    copy_rows = jnp.sum(
        jnp.where(hot_flag[None, :], row_counts, 0).reshape(n_rep, n_rep, n_ep), axis=1, dtype=jnp.int32
    ).reshape(-1)
    served = jnp.where(hot_flag, jnp.zeros_like(counts), counts) + copy_rows
    return served.astype(jnp.float32) / jnp.float32(routed)


def local(tokens, expert_ids, route_weight, hot_plan, gate_proj, up_proj, down_proj):
    n_rep = lax.axis_size("rep")
    n_ep = lax.axis_size("ep")
    devices = n_rep * n_ep
    tok_rows, top = expert_ids.shape
    width = tokens.shape[1]
    routed = tok_rows * top
    hot_cap = max(16, 2 * routed // devices)
    shares = route_weight / jnp.sum(route_weight, axis=1, keepdims=True)
    told = jnp.concatenate([expert_ids.astype(jnp.float32).T, shares.T], axis=0)
    all_told = lax.all_gather(told, AXES)
    all_ids, all_shares = all_told[:, :top], all_told[:, top:]
    served_load = load_of(all_ids, hot_plan, n_rep, n_ep, routed)
    chunks = max(1, devices * tok_rows * width * 2 // (32 * 1024 * 1024))
    rows = tok_rows // chunks
    outs = []
    for i in range(chunks):
        part = slice(i * rows, (i + 1) * rows)
        x = lax.all_gather(tokens[part], AXES)
        y = run_expert(
            x, all_ids[:, :, part], all_shares[:, :, part], gate_proj[0], up_proj[0], down_proj[0], min(hot_cap, rows)
        )
        outs.append(lax.psum_scatter(y, AXES, scatter_dimension=0, tiled=False))
    out = outs[0] if chunks == 1 else jnp.concatenate(outs, axis=0)
    return (out, served_load)


def solution(mesh):
    placed = (
        P(AXES, None),
        P(AXES, None),
        P(AXES, None),
        P(),
        P(AXES, None, None),
        P(AXES, None, None),
        P(AXES, None, None),
    )
    return jax.shard_map(
        local, mesh=mesh, in_specs=placed, out_specs=(P(AXES, None), P()), check_vma=False
    )
```

```python
import functools

import jax
import jax.numpy as jnp
from jax import lax
from jax.experimental import pallas as pl
from jax.experimental.pallas import tpu as pltpu
from jax.sharding import PartitionSpec as P

AXES = ("rep", "ep")


def expert_kernel(cap, ids_ref, share_ref, x_ref, gate_ref, up_ref, down_ref, out_ref, sel, res):
    blocks, top, rows = ids_ref.shape
    me = (lax.axis_index("rep") * lax.axis_size("ep") + lax.axis_index("ep")).astype(jnp.float32)
    earlier = lax.broadcasted_iota(jnp.int32, (rows, rows), 0) < lax.broadcasted_iota(
        jnp.int32, (rows, rows), 1
    )
    earlier = earlier.astype(jnp.bfloat16)
    slots = lax.broadcasted_iota(jnp.int32, (cap, rows), 0).astype(jnp.float32)
    picks = []
    scales = []
    for b in range(blocks):
        match = ids_ref[b] == me
        weight = jnp.sum(jnp.where(match, share_ref[b], 0.0), axis=0, keepdims=True)
        named = jnp.max(match.astype(jnp.float32), axis=0, keepdims=True)
        before = jnp.dot(
            jnp.broadcast_to(named, (8, rows)).astype(jnp.bfloat16),
            earlier,
            preferred_element_type=jnp.float32,
        )[0:1]
        hit = (slots == before) & (named > 0.0)
        pick = jnp.where(hit, 1.0, 0.0)
        picks.append(pick.astype(jnp.bfloat16))
        scales.append(jnp.sum(pick * weight, axis=1, keepdims=True))
        sel[b * cap : (b + 1) * cap, :] = jnp.dot(
            picks[b], x_ref[b], preferred_element_type=jnp.float32
        ).astype(jnp.bfloat16)
    gate_in = jnp.dot(sel[...], gate_ref[...], preferred_element_type=jnp.float32)
    up_in = jnp.dot(sel[...], up_ref[...], preferred_element_type=jnp.float32)
    hidden = (gate_in / (1.0 + jnp.exp(-gate_in)) * up_in).astype(jnp.bfloat16)
    done = jnp.dot(hidden, down_ref[...], preferred_element_type=jnp.float32)
    for b in range(blocks):
        part = slice(b * cap, (b + 1) * cap)
        res[part, :] = (done[part] * scales[b]).astype(jnp.bfloat16)
    for b in range(blocks):
        out_ref[b] = lax.dot_general(
            picks[b],
            res[b * cap : (b + 1) * cap, :],
            (((0,), (0,)), ((), ())),
            preferred_element_type=jnp.float32,
        ).astype(jnp.bfloat16)


def run_expert(x, ids, shares, gate, up, down, cap):
    blocks, rows, width = x.shape
    top = ids.shape[1]
    hidden = gate.shape[1]
    group = 8 if blocks % 8 == 0 else 1
    whole = lambda shape: pl.BlockSpec(shape, lambda i: (0, 0), pipeline_mode=pl.Buffered(1))
    return pl.pallas_call(
        functools.partial(expert_kernel, cap),
        out_shape=jax.ShapeDtypeStruct(x.shape, jnp.bfloat16),
        grid=(blocks // group,),
        in_specs=[
            pl.BlockSpec((group, top, rows), lambda i: (i, 0, 0)),
            pl.BlockSpec((group, top, rows), lambda i: (i, 0, 0)),
            pl.BlockSpec((group, rows, width), lambda i: (i, 0, 0)),
            whole(gate.shape),
            whole(up.shape),
            whole(down.shape),
        ],
        out_specs=pl.BlockSpec((group, rows, width), lambda i: (i, 0, 0)),
        scratch_shapes=[
            pltpu.VMEM((group * cap, width), jnp.bfloat16),
            pltpu.VMEM((group * cap, width), jnp.bfloat16),
        ],
        compiler_params=pltpu.CompilerParams(vmem_limit_bytes=56 * 1024 * 1024),
        cost_estimate=pl.CostEstimate(
            flops=6 * blocks * cap * width * hidden,
            bytes_accessed=4 * blocks * rows * width + 6 * width * hidden,
            transcendentals=blocks * cap * hidden,
        ),
    )(ids, shares, x, gate, up, down)


def sum_kernel(y_ref, out_ref, held, r0, r1a, r1b, r2a, r2b, from_left, from_right, load, send, recv):
    n_z, rows, width = y_ref.shape[2], y_ref.shape[4], y_ref.shape[5]
    half = width // 2
    rep, ep = lax.axis_index("rep"), lax.axis_index("ep")
    x, core, z, y = rep // 2, rep % 2, ep // 2, ep % 2
    ox, oy = 1 - x, 1 - y
    to_core = (2 * x + 1 - core, ep)
    to_x = (2 * ox + core, ep)
    to_y = (rep, 2 * z + oy)
    to_left = (rep, (ep + 2 * n_z - 2) % (2 * n_z))
    to_right = (rep, (ep + 2) % (2 * n_z))
    left, right = pl.ds(0, half), pl.ds(half, half)

    barrier = pltpu.get_barrier_semaphore()

    def greet(who):
        pl.semaphore_signal(barrier, inc=1, device_id=who, device_id_type=pl.DeviceIdType.MESH)

    greet(to_core)
    greet(to_x)
    greet(to_y)

    @pl.when(z > 0)
    def _():
        greet(to_left)

    @pl.when(z < n_z - 1)
    def _():
        greet(to_right)

    peers = 3 + (z > 0).astype(jnp.int32) + (z < n_z - 1).astype(jnp.int32)
    pl.semaphore_wait(barrier, peers)

    def remote(src, dst, kind, k, who):
        return pltpu.make_async_remote_copy(
            src_ref=src,
            dst_ref=dst,
            send_sem=send.at[kind, k],
            recv_sem=recv.at[kind, k],
            device_id=who,
            device_id_type=pl.DeviceIdType.MESH,
        )

    def copy_core(k):
        return remote(y_ref.at[:, 1 - core, k], r0.at[k], 0, k, to_core)

    def copy_own(k):
        return pltpu.make_async_copy(y_ref.at[:, core, k], held.at[k], load.at[k])

    def copies_1(k):
        return (
            remote(held.at[k, ox, :, :, left], r1a.at[k], 1, k, to_x),
            remote(held.at[k, :, oy, :, right], r1b.at[k], 2, k, to_y),
        )

    def copies_2(k):
        return (
            remote(held.at[k, x, oy, :, left], r2a.at[k], 3, k, to_y),
            remote(held.at[k, ox, y, :, right], r2b.at[k], 4, k, to_x),
        )

    def copy_right(k):
        return remote(held.at[k, x, y], from_left.at[k], 5, k, to_right)

    def copy_left(k):
        return remote(held.at[k, x, y], from_right.at[k], 6, k, to_left)

    step = 16

    def over_rows(body):
        @pl.loop(0, rows // step)
        def _(i):
            body(pl.ds(pl.multiple_of(i * step, step), step))

    def take_core(k):
        copy_own(k).wait()
        copy_core(k).wait_recv()

        def body(at):
            for i in range(2):
                for j in range(2):
                    held[k, i, j, at, :] = held[k, i, j, at, :] + r0[k, i, j, at, :]

        over_rows(body)
        for c in copies_1(k):
            c.start()

    def take_1(k):
        for c in copies_1(k):
            c.wait_recv()

        def body(at):
            for i in range(2):
                held[k, x, i, at, left] = held[k, x, i, at, left] + r1a[k, i, at, :]
                held[k, i, y, at, right] = held[k, i, y, at, right] + r1b[k, i, at, :]

        over_rows(body)
        for c in copies_2(k):
            c.start()

    def take_2(k):
        for c in copies_2(k):
            c.wait_recv()

        def body(at):
            held[k, x, y, at, left] = held[k, x, y, at, left] + r2a[k, at, :]
            held[k, x, y, at, right] = held[k, x, y, at, right] + r2b[k, at, :]

        over_rows(body)

    def take_z(k):
        if k > 0:

            @pl.when((z > 0) & (z <= k))
            def _():
                copy_right(k).wait_recv()

                def body(at):
                    held[k, x, y, at, :] = held[k, x, y, at, :] + from_left[k, at, :]

                over_rows(body)

            @pl.when(z < k)
            def _():
                copy_right(k).start()

        if k < n_z - 1:

            @pl.when((z < n_z - 1) & (z >= k))
            def _():
                copy_left(k).wait_recv()

                def body(at):
                    held[k, x, y, at, :] = held[k, x, y, at, :] + from_right[k, at, :]

                over_rows(body)

            @pl.when(z > k)
            def _():
                copy_left(k).start()

        @pl.when(z == k)
        def _():
            def body(at):
                out_ref[at, :] = held[k, x, y, at, :]

            over_rows(body)

    order = []
    for k in range((n_z + 1) // 2):
        order += [n_z - 1 - k, k] if n_z - 1 - k != k else [k]
    for k in order:
        copy_core(k).start()
        copy_own(k).start()
    for t in range(n_z + 3):
        for late, stage in enumerate((take_core, take_1, take_2, take_z)):
            if 0 <= t - late < n_z:
                stage(order[t - late])
    for k in order:
        copy_core(k).wait_send()
        for c in copies_1(k) + copies_2(k):
            c.wait_send()
        if k > 0:

            @pl.when(z < k)
            def _():
                copy_right(k).wait_send()

        if k < n_z - 1:

            @pl.when(z > k)
            def _():
                copy_left(k).wait_send()


def sum_blocks(y, n_rep, n_ep):
    rows, width = y.shape[1:]
    n_z, half = n_ep // 2, width // 2
    assert n_rep == 4 and n_ep % 2 == 0
    vmem = lambda *shape: pltpu.VMEM(shape, jnp.bfloat16)
    return pl.pallas_call(
        sum_kernel,
        out_shape=jax.ShapeDtypeStruct((rows, width), jnp.bfloat16),
        in_specs=[pl.BlockSpec(memory_space=pl.ANY)],
        out_specs=pl.BlockSpec(memory_space=pltpu.VMEM),
        scratch_shapes=[
            vmem(n_z, 2, 2, rows, width),
            vmem(n_z, 2, 2, rows, width),
            vmem(n_z, 2, rows, half),
            vmem(n_z, 2, rows, half),
            vmem(n_z, rows, half),
            vmem(n_z, rows, half),
            vmem(n_z, rows, width),
            vmem(n_z, rows, width),
            pltpu.SemaphoreType.DMA((n_z,)),
            pltpu.SemaphoreType.DMA((7, n_z)),
            pltpu.SemaphoreType.DMA((7, n_z)),
        ],
        compiler_params=pltpu.CompilerParams(
            collective_id=0, has_side_effects=True, vmem_limit_bytes=56 * 1024 * 1024
        ),
    )(y.reshape(2, 2, n_z, 2, rows, width))


def load_of(all_ids, hot_plan, n_rep, n_ep, routed):
    devices = n_rep * n_ep
    expert_range = jnp.arange(devices, dtype=jnp.int32)
    by_row = all_ids.reshape(n_rep, 1, -1)
    row_counts = jnp.sum(
        (by_row == expert_range.astype(jnp.float32)[None, :, None]).astype(jnp.float32), axis=2
    ).astype(jnp.int32)
    hot_flag = (expert_range // n_ep) == jnp.tile(hot_plan, n_rep)
    counts = jnp.sum(row_counts, axis=0, dtype=jnp.int32)
    copy_rows = jnp.sum(
        jnp.where(hot_flag[None, :], row_counts, 0).reshape(n_rep, n_rep, n_ep), axis=1, dtype=jnp.int32
    ).reshape(-1)
    served = jnp.where(hot_flag, jnp.zeros_like(counts), counts) + copy_rows
    return served.astype(jnp.float32) / jnp.float32(routed)


def local(tokens, expert_ids, route_weight, hot_plan, gate_proj, up_proj, down_proj):
    n_rep = lax.axis_size("rep")
    n_ep = lax.axis_size("ep")
    devices = n_rep * n_ep
    tok_rows, top = expert_ids.shape
    width = tokens.shape[1]
    routed = tok_rows * top
    hot_cap = max(16, 2 * routed // devices)
    shares = route_weight / jnp.sum(route_weight, axis=1, keepdims=True)
    told = jnp.concatenate([expert_ids.astype(jnp.float32).T, shares.T], axis=0)
    all_told = lax.all_gather(told, AXES)
    all_ids, all_shares = all_told[:, :top], all_told[:, top:]
    served_load = load_of(all_ids, hot_plan, n_rep, n_ep, routed)
    chunks = max(1, devices * tok_rows * width * 2 // (16 * 1024 * 1024))
    rows = tok_rows // chunks
    outs = []
    for i in range(chunks):
        part = slice(i * rows, (i + 1) * rows)
        x = lax.all_gather(tokens[part], AXES)
        y = run_expert(
            x, all_ids[:, :, part], all_shares[:, :, part], gate_proj[0], up_proj[0], down_proj[0], min(hot_cap, rows)
        )
        outs.append(sum_blocks(y, n_rep, n_ep))
    out = outs[0] if chunks == 1 else jnp.concatenate(outs, axis=0)
    return (out, served_load)


def solution(mesh):
    placed = (
        P(AXES, None),
        P(AXES, None),
        P(AXES, None),
        P(),
        P(AXES, None, None),
        P(AXES, None, None),
        P(AXES, None, None),
    )
    return jax.shard_map(
        local, mesh=mesh, in_specs=placed, out_specs=(P(AXES, None), P()), check_vma=False
    )
```

```python
import functools

import jax
import jax.numpy as jnp
from jax import lax
from jax.experimental import pallas as pl
from jax.experimental.pallas import tpu as pltpu
from jax.sharding import PartitionSpec as P

AXES = ("rep", "ep")


def expert_kernel(cap, ids_ref, share_ref, x_ref, gate_ref, up_ref, down_ref, out_ref, sel, res):
    blocks, top, rows = ids_ref.shape
    me = (lax.axis_index("rep") * lax.axis_size("ep") + lax.axis_index("ep")).astype(jnp.float32)
    earlier = lax.broadcasted_iota(jnp.int32, (rows, rows), 0) < lax.broadcasted_iota(
        jnp.int32, (rows, rows), 1
    )
    earlier = earlier.astype(jnp.bfloat16)
    pair = 2 if blocks % 2 == 0 else 1
    places = lax.broadcasted_iota(jnp.int32, (pair * cap, pair * rows), 0).astype(jnp.float32)
    picks = []
    scales = []
    for p in range(blocks // pair):
        targets = []
        weights = []
        for q in range(pair):
            match = ids_ref[p * pair + q] == me
            weights.append(jnp.sum(jnp.where(match, share_ref[p * pair + q], 0.0), axis=0, keepdims=True))
            named = jnp.max(match.astype(jnp.float32), axis=0, keepdims=True)
            before = jnp.dot(
                jnp.broadcast_to(named, (8, rows)).astype(jnp.bfloat16),
                earlier,
                preferred_element_type=jnp.float32,
            )[0:1]
            targets.append(jnp.where(named > 0.0, before + q * cap, -1.0))
        pick = jnp.where(places == jnp.concatenate(targets, axis=1), 1.0, 0.0)
        picks.append(pick.astype(jnp.bfloat16))
        scales.append(jnp.sum(pick * jnp.concatenate(weights, axis=1), axis=1, keepdims=True))
        sel[p * pair * cap : (p + 1) * pair * cap, :] = jnp.dot(
            picks[p],
            x_ref[p * pair : (p + 1) * pair].reshape(pair * rows, x_ref.shape[2]),
            preferred_element_type=jnp.float32,
        ).astype(jnp.bfloat16)
    gate_in = jnp.dot(sel[...], gate_ref[...], preferred_element_type=jnp.float32)
    up_in = jnp.dot(sel[...], up_ref[...], preferred_element_type=jnp.float32)
    hidden = (gate_in / (1.0 + jnp.exp(-gate_in)) * up_in).astype(jnp.bfloat16)
    scale = jnp.concatenate(scales, axis=0)
    width = x_ref.shape[2]
    part = width // 4 if width % 512 == 0 else width
    for at in range(0, width, part):
        done = jnp.dot(hidden, down_ref[:, at : at + part], preferred_element_type=jnp.float32)
        res[:, at : at + part] = (done * scale).astype(jnp.bfloat16)
        for p in range(blocks // pair):
            out_ref[p * pair : (p + 1) * pair, :, at : at + part] = (
                lax.dot_general(
                    picks[p],
                    res[p * pair * cap : (p + 1) * pair * cap, at : at + part],
                    (((0,), (0,)), ((), ())),
                    preferred_element_type=jnp.float32,
                )
                .astype(jnp.bfloat16)
                .reshape(pair, rows, part)
            )


def run_expert(x, ids, shares, gate, up, down, cap):
    blocks, rows, width = x.shape
    top = ids.shape[1]
    hidden = gate.shape[1]
    group = 8 if blocks % 8 == 0 else 1
    whole = lambda shape: pl.BlockSpec(shape, lambda i: (0, 0), pipeline_mode=pl.Buffered(1))
    return pl.pallas_call(
        functools.partial(expert_kernel, cap),
        out_shape=jax.ShapeDtypeStruct(x.shape, jnp.bfloat16),
        grid=(blocks // group,),
        in_specs=[
            pl.BlockSpec((group, top, rows), lambda i: (i, 0, 0)),
            pl.BlockSpec((group, top, rows), lambda i: (i, 0, 0)),
            pl.BlockSpec((group, rows, width), lambda i: (i, 0, 0)),
            whole(gate.shape),
            whole(up.shape),
            whole(down.shape),
        ],
        out_specs=pl.BlockSpec((group, rows, width), lambda i: (i, 0, 0)),
        scratch_shapes=[
            pltpu.VMEM((group * cap, width), jnp.bfloat16),
            pltpu.VMEM((group * cap, width), jnp.bfloat16),
        ],
        compiler_params=pltpu.CompilerParams(vmem_limit_bytes=56 * 1024 * 1024),
        cost_estimate=pl.CostEstimate(
            flops=6 * blocks * cap * width * hidden,
            bytes_accessed=4 * blocks * rows * width + 6 * width * hidden,
            transcendentals=blocks * cap * hidden,
        ),
    )(ids, shares, x, gate, up, down)


def sum_kernel(y_ref, out_ref, held, r0, r1a, r1b, r2a, r2b, from_left, from_right, load, send, recv):
    n_z, rows, width = y_ref.shape[2], y_ref.shape[4], y_ref.shape[5]
    half = width // 2
    rep, ep = lax.axis_index("rep"), lax.axis_index("ep")
    x, core, z, y = rep // 2, rep % 2, ep // 2, ep % 2
    ox, oy = 1 - x, 1 - y
    to_core = (2 * x + 1 - core, ep)
    to_x = (2 * ox + core, ep)
    to_y = (rep, 2 * z + oy)
    to_left = (rep, (ep + 2 * n_z - 2) % (2 * n_z))
    to_right = (rep, (ep + 2) % (2 * n_z))
    left, right = pl.ds(0, half), pl.ds(half, half)

    barrier = pltpu.get_barrier_semaphore()

    def greet(who):
        pl.semaphore_signal(barrier, inc=1, device_id=who, device_id_type=pl.DeviceIdType.MESH)

    greet(to_core)
    greet(to_x)
    greet(to_y)

    @pl.when(z > 0)
    def _():
        greet(to_left)

    @pl.when(z < n_z - 1)
    def _():
        greet(to_right)

    peers = 3 + (z > 0).astype(jnp.int32) + (z < n_z - 1).astype(jnp.int32)
    pl.semaphore_wait(barrier, peers)

    def remote(src, dst, kind, k, who):
        return pltpu.make_async_remote_copy(
            src_ref=src,
            dst_ref=dst,
            send_sem=send.at[kind, k],
            recv_sem=recv.at[kind, k],
            device_id=who,
            device_id_type=pl.DeviceIdType.MESH,
        )

    def copy_core(k):
        return remote(y_ref.at[:, 1 - core, k], r0.at[k], 0, k, to_core)

    def copy_own(k):
        return pltpu.make_async_copy(y_ref.at[:, core, k], held.at[k], load.at[k])

    def copies_1(k):
        return (
            remote(held.at[k, ox, :, :, left], r1a.at[k], 1, k, to_x),
            remote(held.at[k, :, oy, :, right], r1b.at[k], 2, k, to_y),
        )

    def copies_2(k):
        return (
            remote(held.at[k, x, oy, :, left], r2a.at[k], 3, k, to_y),
            remote(held.at[k, ox, y, :, right], r2b.at[k], 4, k, to_x),
        )

    def copy_right(k):
        return remote(held.at[k, x, y], from_left.at[k], 5, k, to_right)

    def copy_left(k):
        return remote(held.at[k, x, y], from_right.at[k], 6, k, to_left)

    step = 16

    def over_rows(body):
        @pl.loop(0, rows // step)
        def _(i):
            body(pl.ds(pl.multiple_of(i * step, step), step))

    def take_core(k):
        copy_own(k).wait()
        copy_core(k).wait_recv()

        def body(at):
            for i in range(2):
                for j in range(2):
                    held[k, i, j, at, :] = held[k, i, j, at, :] + r0[k, i, j, at, :]

        over_rows(body)
        for c in copies_1(k):
            c.start()

    def take_1(k):
        for c in copies_1(k):
            c.wait_recv()

        def body(at):
            for i in range(2):
                held[k, x, i, at, left] = held[k, x, i, at, left] + r1a[k, i, at, :]
                held[k, i, y, at, right] = held[k, i, y, at, right] + r1b[k, i, at, :]

        over_rows(body)
        for c in copies_2(k):
            c.start()

    def take_2(k):
        for c in copies_2(k):
            c.wait_recv()

        def body(at):
            held[k, x, y, at, left] = held[k, x, y, at, left] + r2a[k, at, :]
            held[k, x, y, at, right] = held[k, x, y, at, right] + r2b[k, at, :]

        over_rows(body)

    def take_z(k):
        if k > 0:

            @pl.when((z > 0) & (z <= k))
            def _():
                copy_right(k).wait_recv()

                def body(at):
                    held[k, x, y, at, :] = held[k, x, y, at, :] + from_left[k, at, :]

                over_rows(body)

            @pl.when(z < k)
            def _():
                copy_right(k).start()

        if k < n_z - 1:

            @pl.when((z < n_z - 1) & (z >= k))
            def _():
                copy_left(k).wait_recv()

                def body(at):
                    held[k, x, y, at, :] = held[k, x, y, at, :] + from_right[k, at, :]

                over_rows(body)

            @pl.when(z > k)
            def _():
                copy_left(k).start()

        @pl.when(z == k)
        def _():
            def body(at):
                out_ref[at, :] = held[k, x, y, at, :]

            over_rows(body)

    order = []
    for k in range((n_z + 1) // 2):
        order += [n_z - 1 - k, k] if n_z - 1 - k != k else [k]
    for k in order:
        copy_core(k).start()
        copy_own(k).start()
    for t in range(n_z + 3):
        for late, stage in enumerate((take_core, take_1, take_2, take_z)):
            if 0 <= t - late < n_z:
                stage(order[t - late])
    for k in order:
        copy_core(k).wait_send()
        for c in copies_1(k) + copies_2(k):
            c.wait_send()
        if k > 0:

            @pl.when(z < k)
            def _():
                copy_right(k).wait_send()

        if k < n_z - 1:

            @pl.when(z > k)
            def _():
                copy_left(k).wait_send()


def sum_blocks(y, n_rep, n_ep):
    rows, width = y.shape[1:]
    n_z, half = n_ep // 2, width // 2
    assert n_rep == 4 and n_ep % 2 == 0
    vmem = lambda *shape: pltpu.VMEM(shape, jnp.bfloat16)
    return pl.pallas_call(
        sum_kernel,
        out_shape=jax.ShapeDtypeStruct((rows, width), jnp.bfloat16),
        in_specs=[pl.BlockSpec(memory_space=pl.ANY)],
        out_specs=pl.BlockSpec(memory_space=pltpu.VMEM),
        scratch_shapes=[
            vmem(n_z, 2, 2, rows, width),
            vmem(n_z, 2, 2, rows, width),
            vmem(n_z, 2, rows, half),
            vmem(n_z, 2, rows, half),
            vmem(n_z, rows, half),
            vmem(n_z, rows, half),
            vmem(n_z, rows, width),
            vmem(n_z, rows, width),
            pltpu.SemaphoreType.DMA((n_z,)),
            pltpu.SemaphoreType.DMA((7, n_z)),
            pltpu.SemaphoreType.DMA((7, n_z)),
        ],
        compiler_params=pltpu.CompilerParams(
            collective_id=0, has_side_effects=True, vmem_limit_bytes=56 * 1024 * 1024
        ),
    )(y.reshape(2, 2, n_z, 2, rows, width))


def load_of(all_ids, hot_plan, n_rep, n_ep, routed):
    devices = n_rep * n_ep
    expert_range = jnp.arange(devices, dtype=jnp.int32)
    by_row = all_ids.reshape(n_rep, 1, -1)
    row_counts = jnp.sum(
        (by_row == expert_range.astype(jnp.float32)[None, :, None]).astype(jnp.float32), axis=2
    ).astype(jnp.int32)
    hot_flag = (expert_range // n_ep) == jnp.tile(hot_plan, n_rep)
    counts = jnp.sum(row_counts, axis=0, dtype=jnp.int32)
    copy_rows = jnp.sum(
        jnp.where(hot_flag[None, :], row_counts, 0).reshape(n_rep, n_rep, n_ep), axis=1, dtype=jnp.int32
    ).reshape(-1)
    served = jnp.where(hot_flag, jnp.zeros_like(counts), counts) + copy_rows
    return served.astype(jnp.float32) / jnp.float32(routed)


def local(tokens, expert_ids, route_weight, hot_plan, gate_proj, up_proj, down_proj):
    n_rep = lax.axis_size("rep")
    n_ep = lax.axis_size("ep")
    devices = n_rep * n_ep
    tok_rows, top = expert_ids.shape
    width = tokens.shape[1]
    routed = tok_rows * top
    hot_cap = max(16, 2 * routed // devices)
    shares = route_weight / jnp.sum(route_weight, axis=1, keepdims=True)
    told = jnp.concatenate([expert_ids.astype(jnp.float32).T, shares.T], axis=0)
    all_told = lax.all_gather(told, AXES)
    all_ids, all_shares = all_told[:, :top], all_told[:, top:]
    served_load = load_of(all_ids, hot_plan, n_rep, n_ep, routed)
    chunks = max(1, devices * tok_rows * width * 2 // (16 * 1024 * 1024))
    rows = tok_rows // chunks
    outs = []
    for i in range(chunks):
        part = slice(i * rows, (i + 1) * rows)
        x = lax.all_gather(tokens[part], AXES)
        y = run_expert(
            x, all_ids[:, :, part], all_shares[:, :, part], gate_proj[0], up_proj[0], down_proj[0], min(hot_cap, rows)
        )
        outs.append(sum_blocks(y, n_rep, n_ep))
    out = outs[0] if chunks == 1 else jnp.concatenate(outs, axis=0)
    return (out, served_load)


def solution(mesh):
    placed = (
        P(AXES, None),
        P(AXES, None),
        P(AXES, None),
        P(),
        P(AXES, None, None),
        P(AXES, None, None),
        P(AXES, None, None),
    )
    return jax.shard_map(
        local, mesh=mesh, in_specs=placed, out_specs=(P(AXES, None), P()), check_vma=False
    )
```
